32 devices in a mesh: seq: 8 (over z, core), head: 4 (over y, x).
Axes of the slice: x: 2, y: 2, z: 4, core: 2. Of those that a mesh axis runs over, the one named last changes fastest.
Arguments:
- queries: bfloat16 [2048, 16384], P('seq', 'head'), may hold values from -8 to 8
- keys: bfloat16 [2048, 1024], P('seq'), may hold values from -8 to 8
- values: bfloat16 [2048, 1024], P('seq'), may hold values from -8 to 8
- query_map: bfloat16 [128, 128, 128], P('head'), may hold values from -3 to 3
- key_map: bfloat16 [8, 128, 128], replicated, may hold values from -3 to 3
- positions: int32 [2048], P('seq'), may hold values from 0 to 131071, as said below
Outputs:
- error_grad: bfloat16 [2048, 16384], P('seq', 'head')
The draws below stay inside these ranges and needn't reach their ends.
Inputs may be any that keep to these rules, and one draw needn't show every extreme that they name: `positions`: each token's position is one more than the token before it, or 0 where a new document begins; the window begins inside a document that ends at position 131071, and at least one document begins inside the window.
All inputs are finite; a program needn't handle non-finite values.
Results may differ from the reference program's by a relative error of at most 0.0085.
Values may be sent and summed in bfloat16 or wider, within the bound.
A program may use at most 128 MiB of HBM per device.

```python
import math
import jax
import jax.numpy as jnp
from jax import lax

HD = 128
QHEADS = 128
KVH = 8
LENGTH = 131072
SEQ = 2048


feature_shift = 3.0


feature_spread = 2.0


def common_plan(key):
    folded_key = jax.random.fold_in(key, 5151)
    key_one, key_two = jax.random.split(folded_key)
    key_signs = (jax.random.randint(key_one, (KVH, HD), 0, 2) * 2 - 1).astype(jnp.float32)
    query_signs = (jax.random.randint(key_two, (QHEADS, HD), 0, 2) * 2 - 1).astype(jnp.float32)
    return (key_signs, query_signs)


def structured_map(key, signs):
    count = signs.shape[0]
    gaussian = jax.random.normal(key, (count, HD, HD), jnp.float32)
    orthogonal, unused = jnp.linalg.qr(gaussian)
    projector = jnp.eye(HD, dtype=jnp.float32)[None] - signs[:, :, None] * signs[:, None, :] / HD
    rotated = jnp.einsum('gij,gjk->gik', projector, orthogonal, precision=lax.Precision.HIGHEST)
    shifted = feature_shift / HD * signs[:, :, None] * jnp.ones((1, 1, HD), jnp.float32)
    return feature_spread * rotated - shifted


def base_keys(key):
    full_shape = (SEQ, KVH * HD)
    own_key = jax.random.fold_in(key, 17)
    key_signs, query_signs = common_plan(key)
    noise = jnp.clip(jax.random.normal(own_key, full_shape, jnp.float32), -6.0, 6.0)
    return noise + key_signs.reshape(1, KVH * HD)


def draw_queries(key, part):
    full_shape = (SEQ, QHEADS * HD)
    key_signs, query_signs = common_plan(key)
    drawn = jnp.clip(jax.random.normal(key, full_shape, jnp.float32), -6.0, 6.0) + query_signs.reshape(1, QHEADS * HD)
    return drawn.astype(jnp.bfloat16)


def draw_keys(key, part):
    drawn = base_keys(key)
    return drawn.astype(jnp.bfloat16)


def draw_values(key, part):
    keys_base = base_keys(key)
    key_signs, query_signs = common_plan(key)
    key_maps = structured_map(jax.random.fold_in(key, 31), key_signs)
    projected = jnp.einsum('tgd,gde->tge', keys_base.reshape(SEQ, KVH, HD), key_maps, precision=lax.Precision.HIGHEST)
    noise_key = jax.random.fold_in(key, 53)
    noise = 0.5 * jax.random.normal(noise_key, (SEQ, KVH, HD), jnp.float32)
    drawn = (projected + feature_shift) / feature_spread + noise
    return jnp.clip(drawn, -8.0, 8.0).reshape(SEQ, KVH * HD).astype(jnp.bfloat16)


def draw_key_map(key, part):
    key_signs, query_signs = common_plan(key)
    return structured_map(jax.random.fold_in(key, 31), key_signs).astype(jnp.bfloat16)


def draw_query_map(key, part):
    key_signs, query_signs = common_plan(key)
    return structured_map(jax.random.fold_in(key, 37), query_signs).astype(jnp.bfloat16)


def draw_positions(key, part):
    key_break, key_first = jax.random.split(jax.random.fold_in(key, 99))
    token_order = jnp.arange(SEQ, dtype=jnp.int32)
    first_break = jax.random.randint(key_first, (), 1, SEQ)
    random_breaks = jax.random.randint(key_break, (SEQ,), 0, 1024) == 0
    breaks = random_breaks & (token_order > first_break) | (token_order == first_break)
    latest = lax.cummax(jnp.where(breaks, token_order, 0), axis=0)
    return jnp.where(token_order < first_break, LENGTH - first_break + token_order, token_order - latest).astype(jnp.int32)


def setup_inputs(seed: int = 0) -> dict:
    seeds = jax.random.split(jax.random.key(seed), 7)
    queries = draw_queries(jax.random.fold_in(seeds[6], 71), 0)
    keys = draw_keys(jax.random.fold_in(seeds[6], 71), 0)
    values = draw_values(jax.random.fold_in(seeds[6], 71), 0)
    query_map = draw_query_map(jax.random.fold_in(seeds[6], 71), 0)
    key_map = draw_key_map(jax.random.fold_in(seeds[6], 71), 0)
    positions = draw_positions(jax.random.fold_in(seeds[6], 71), 0)
    return dict(queries=queries, keys=keys, values=values, query_map=query_map, key_map=key_map, positions=positions)


epsilon = 1e-06
masked_score = -1e+30
highest = lax.Precision.HIGHEST

def reference(queries, keys, values, query_map, key_map, positions):
    group_size = QHEADS // KVH
    angles = 0.5 * math.pi / LENGTH * positions.astype(jnp.float32)
    cosine_part = jnp.cos(angles)[:, None]
    sine_part = jnp.sin(angles)[:, None]
    token_order = jnp.arange(SEQ, dtype=jnp.int32)
    causal = token_order[:, None] >= token_order[None, :]
    scaling = 1.0 / math.sqrt(HD)
    block_rows = math.gcd(512, SEQ)
    blocks = SEQ // block_rows
    inside = jnp.arange(block_rows)[:, None] >= jnp.arange(block_rows)[None, :]

    def key_features(group_index):
        group_keys = lax.dynamic_slice_in_dim(keys, group_index * HD, HD, 1)
        mapped = jax.nn.elu(jnp.dot(group_keys.astype(jnp.float32), key_map[group_index].astype(jnp.float32), preferred_element_type=jnp.float32)) + 1.0
        return jnp.concatenate([cosine_part * mapped, sine_part * mapped], axis=1).astype(jnp.bfloat16)
    key_feats = lax.map(key_features, jnp.arange(KVH, dtype=jnp.int32))

    def one_head(head_index):
        group_index = head_index // group_size
        head_queries = lax.dynamic_slice_in_dim(queries, head_index * HD, HD, 1)
        head_keys = lax.dynamic_slice_in_dim(keys, group_index * HD, HD, 1)
        head_values = lax.dynamic_slice_in_dim(values, group_index * HD, HD, 1)
        scores = jnp.dot(head_queries.astype(jnp.float32), head_keys.T.astype(jnp.float32), preferred_element_type=jnp.float32) * scaling
        scores = jnp.where(causal, scores, masked_score)
        largest = lax.optimization_barrier(jnp.max(scores, axis=1, keepdims=True))
        weights = jnp.where(causal, jnp.exp(scores - largest), 0.0)
        weight_total = lax.optimization_barrier(jnp.sum(weights, axis=1, keepdims=True))
        teacher = (jnp.dot(weights.astype(jnp.bfloat16).astype(jnp.float32), head_values.astype(jnp.float32), preferred_element_type=jnp.float32) / weight_total).astype(jnp.bfloat16)
        mapped = jax.nn.elu(jnp.dot(head_queries.astype(jnp.float32), query_map[head_index].astype(jnp.float32), preferred_element_type=jnp.float32)) + 1.0
        query_feats = jnp.concatenate([cosine_part * mapped, sine_part * mapped], axis=1).astype(jnp.bfloat16)
        query_rows = query_feats.astype(jnp.float32).reshape(blocks, block_rows, 2 * HD)
        group_feats = key_feats[group_index].astype(jnp.float32).reshape(blocks, block_rows, 2 * HD)
        value_rows = head_values.astype(jnp.float32).reshape(blocks, block_rows, HD)
        totals = jnp.einsum('bjf,bjd->bfd', group_feats, value_rows, precision=highest)
        masses = lax.optimization_barrier(jnp.sum(group_feats, axis=1))
        before = jnp.concatenate([jnp.zeros((1, 2 * HD, HD), jnp.float32), jnp.cumsum(totals, axis=0)[:-1]], axis=0)
        mass_before = jnp.concatenate([jnp.zeros((1, 2 * HD), jnp.float32), jnp.cumsum(masses, axis=0)[:-1]], axis=0)
        inner_block = jnp.where(inside, jnp.einsum('bif,bjf->bij', query_rows, group_feats, precision=highest), 0.0)
        numerator = jnp.einsum('bij,bjd->bid', inner_block, value_rows, precision=highest) + jnp.einsum('bif,bfd->bid', query_rows, before, precision=highest)
        denominator = lax.optimization_barrier(jnp.sum(inner_block, axis=2)) + jnp.einsum('bif,bf->bi', query_rows, mass_before, precision=highest)
        student = (numerator / (denominator[..., None] + epsilon)).reshape(SEQ, HD)
        return (2.0 * (student - teacher.astype(jnp.float32))).astype(jnp.bfloat16)
    gradient = lax.map(one_head, jnp.arange(QHEADS, dtype=jnp.int32))
    return jnp.transpose(gradient, (1, 0, 2)).reshape(SEQ, QHEADS * HD)
```

```python
import functools
import math

import jax
import jax.numpy as jnp
from jax import lax
from jax.experimental import pallas as pl
from jax.experimental.pallas import tpu as pltpu
from jax.sharding import PartitionSpec as P

QHEADS = 128
KVH = 8
LENGTH = 131072
epsilon = 1e-06
masked_score = -1e30
MESH = pl.DeviceIdType.MESH
LOG2E = 1.4426950408889634


def elu_plus_one(x):
    return jnp.where(x > 0.0, x + 1.0, jnp.exp2(jnp.minimum(x, 0.0) * LOG2E))


def angle_parts(positions):
    angles = (0.5 * math.pi / LENGTH) * positions.astype(jnp.float32)
    return jnp.cos(angles), jnp.sin(angles)


def nt_dot(a, b):
    return lax.dot_general(a, b, (((1,), (1,)), ((), ())), preferred_element_type=jnp.float32)


def nn_dot(a, b):
    return jnp.dot(a, b, preferred_element_type=jnp.float32)


def kernel(
    n, kv_local, per_group, unroll,
    q_ref, k_ref, v_ref, qmap_ref, kmap_ref, pos_ref, out_ref,
    kbuf, vbuf, pbuf, acc, top, cat, state, cosq, sinq,
    send_sem, recv_sem, fwd_sem,
):
    tokens = q_ref.shape[0]
    hd = qmap_ref.shape[1]
    heads = qmap_ref.shape[0]
    nz = n // 2
    me = lax.axis_index("seq")
    z = me // 2
    core = me % 2
    partner = z * 2 + 1 - core
    group0 = lax.axis_index("head") * heads // (QHEADS // KVH)
    width = kv_local * hd
    columns = pl.ds(pl.multiple_of(group0 * hd, hd), width)
    scaling = LOG2E / math.sqrt(hd)

    barrier = pltpu.get_barrier_semaphore()

    def greet(zp, carry):
        pl.semaphore_signal(barrier, inc=1, device_id={"seq": zp * 2 + core}, device_id_type=MESH)
        return carry

    lax.fori_loop(0, z, greet, 0)
    lax.fori_loop(z + 1, nz, greet, 0)
    pl.semaphore_signal(barrier, inc=1, device_id={"seq": partner}, device_id_type=MESH)
    pl.semaphore_wait(barrier, nz)

    own = (k_ref.at[:, columns], v_ref.at[:, columns], pos_ref)
    buffers = (kbuf, vbuf, pbuf)

    def own_copy(part, slot, target):
        return pltpu.make_async_remote_copy(
            src_ref=own[part], dst_ref=buffers[part].at[me],
            send_sem=send_sem.at[part, slot], recv_sem=recv_sem.at[part, me],
            device_id={"seq": target}, device_id_type=MESH,
        )

    def forward_copy(part, zp):
        block = zp * 2 + core
        return pltpu.make_async_remote_copy(
            src_ref=buffers[part].at[block], dst_ref=buffers[part].at[block],
            send_sem=fwd_sem.at[part, zp], recv_sem=recv_sem.at[part, block],
            device_id={"seq": partner}, device_id_type=MESH,
        )

    def arrival(part, block):
        return pltpu.make_async_remote_copy(
            src_ref=buffers[part].at[block], dst_ref=buffers[part].at[block],
            send_sem=send_sem.at[part, 0], recv_sem=recv_sem.at[part, block],
            device_id={"seq": partner}, device_id_type=MESH,
        )

    @pl.when(core == 0)
    def _():
        for part in range(3):
            own_copy(part, z, partner).start()

    def send_up(zp, carry):
        for part in range(3):
            own_copy(part, zp, zp * 2 + core).start()
        return carry

    lax.fori_loop(z + 1, nz, send_up, 0)

    ones = jnp.ones((tokens, hd), jnp.bfloat16)

    def key_feats(keys, group, positions):
        cosine, sine = angle_parts(positions)
        projected = nn_dot(keys, kmap_ref[group0 + group]).T
        mapped = elu_plus_one(projected)
        return jnp.concatenate([cosine * mapped, sine * mapped], axis=0).astype(jnp.bfloat16)

    tall = jnp.broadcast_to(pos_ref[...].astype(jnp.float32), (hd, tokens)).T
    cosine, sine = angle_parts(tall)
    cosq[...] = cosine
    sinq[...] = sine
    for g in range(kv_local):
        own_cols = pl.ds(pl.multiple_of((group0 + g) * hd, hd), hd)
        keys = k_ref[:, own_cols]
        values = jnp.concatenate([v_ref[:, own_cols], ones], axis=1)
        feats = key_feats(keys, g, pos_ref[...])
        state[g] = jnp.zeros((2 * hd, 2 * hd), jnp.float32)

        def own_body(i, carry, g=g, keys=keys, values=values, feats=feats):
            row = lax.broadcasted_iota(jnp.int32, (tokens, tokens), 0)
            col = lax.broadcasted_iota(jnp.int32, (tokens, tokens), 1)
            causal = row >= col
            for u in range(unroll):
                h = g * per_group + i * unroll + u
                q = q_ref[:, pl.ds(pl.multiple_of(h * hd, hd), hd)]
                scores = jnp.where(causal, nt_dot(q, keys) * scaling, masked_score)
                largest = jnp.max(scores, axis=1, keepdims=True)
                weights = jnp.exp2(scores - largest).astype(jnp.bfloat16)
                acc[h] = nn_dot(weights, values)
                top[h] = jnp.broadcast_to(largest, (tokens, hd))
                mapped = elu_plus_one(nn_dot(q, qmap_ref[h]))
                qf = jnp.concatenate([cosq[...] * mapped, sinq[...] * mapped], axis=1).astype(jnp.bfloat16)
                inner = jnp.where(causal, nn_dot(qf, feats), 0.0).astype(jnp.bfloat16)
                cat[h, :, :tokens] = inner
                cat[h, :, tokens:] = qf
            return carry

        lax.fori_loop(0, per_group // unroll, own_body, 0)

    def use_block(block):
        for g in range(kv_local):
            group_cols = slice(g * hd, (g + 1) * hd)
            keys = kbuf[block, :, group_cols]
            values = jnp.concatenate([vbuf[block, :, group_cols], ones], axis=1)
            feats = key_feats(keys, g, pbuf[block])
            state[g] += nn_dot(feats, values)

            def body(i, carry, g=g, keys=keys, values=values):
                for u in range(unroll):
                    h = g * per_group + i * unroll + u
                    q = q_ref[:, pl.ds(pl.multiple_of(h * hd, hd), hd)]
                    scores = nt_dot(q, keys) * scaling
                    before = top[h]
                    largest = jnp.maximum(before, jnp.max(scores, axis=1, keepdims=True))
                    factor = jnp.exp2(before - largest)
                    wide = jnp.concatenate([largest] * (tokens // hd), axis=1)
                    weights = jnp.exp2(scores - wide).astype(jnp.bfloat16)
                    acc[h] = acc[h] * jnp.concatenate([factor, factor], axis=1) + nn_dot(weights, values)
                    top[h] = largest
                return carry

            lax.fori_loop(0, per_group // unroll, body, 0)

    @pl.when(core == 1)
    def _():
        for part in range(3):
            arrival(part, partner).wait_recv()
        use_block(partner)

    def step(i, carry):
        zp = z - 1 - i // 2
        first = i % 2 == 0
        block = zp * 2 + jnp.where(first, core, 1 - core)
        for part in range(3):
            arrival(part, block).wait_recv()

        @pl.when(first)
        def _():
            for part in range(3):
                forward_copy(part, zp).start()

        use_block(block)
        return carry

    lax.fori_loop(0, 2 * z, step, 0)

    for g in range(kv_local):
        own_cols = pl.ds(pl.multiple_of((group0 + g) * hd, hd), hd)
        stacked = jnp.concatenate(
            [jnp.concatenate([v_ref[:, own_cols], ones], axis=1), state[g].astype(jnp.bfloat16)], axis=0
        )

        def last_body(i, carry, g=g, stacked=stacked):
            for u in range(unroll):
                h = g * per_group + i * unroll + u
                both = nn_dot(cat[h], stacked)
                student = both[:, :hd] / (both[:, hd:] + epsilon)
                teacher = (acc[h, :, :hd] / acc[h, :, hd:]).astype(jnp.bfloat16).astype(jnp.float32)
                out_ref[:, pl.ds(pl.multiple_of(h * hd, hd), hd)] = (2.0 * (student - teacher)).astype(jnp.bfloat16)
            return carry

        lax.fori_loop(0, per_group // unroll, last_body, 0)

    @pl.when(core == 0)
    def _():
        for part in range(3):
            own_copy(part, z, partner).wait_send()

    def sent(zp, carry):
        for part in range(3):
            own_copy(part, zp, zp * 2 + core).wait_send()
        return carry

    lax.fori_loop(z + 1, nz, sent, 0)

    def forwarded(zp, carry):
        for part in range(3):
            forward_copy(part, zp).wait_send()
        return carry

    lax.fori_loop(0, z, forwarded, 0)


def per_device(n, queries, keys, values, query_map, key_map, positions):
    tokens = queries.shape[0]
    hd = key_map.shape[1]
    heads = query_map.shape[0]
    kv_local = max(1, heads // (QHEADS // KVH))
    per_group = heads // kv_local
    unroll = math.gcd(per_group, 4)
    width = kv_local * hd
    vmem = pl.BlockSpec(memory_space=pltpu.VMEM)
    return pl.pallas_call(
        functools.partial(kernel, n, kv_local, per_group, unroll),
        out_shape=jax.ShapeDtypeStruct(queries.shape, jnp.bfloat16),
        in_specs=[vmem] * 6,
        out_specs=vmem,
        scratch_shapes=[
            pltpu.VMEM((n, tokens, width), jnp.bfloat16),
            pltpu.VMEM((n, tokens, width), jnp.bfloat16),
            pltpu.VMEM((n, 1, tokens), jnp.int32),
            pltpu.VMEM((heads, tokens, 2 * hd), jnp.float32),
            pltpu.VMEM((heads, tokens, hd), jnp.float32),
            pltpu.VMEM((heads, tokens, tokens + 2 * hd), jnp.bfloat16),
            pltpu.VMEM((kv_local, 2 * hd, 2 * hd), jnp.float32),
            pltpu.VMEM((tokens, hd), jnp.float32),
            pltpu.VMEM((tokens, hd), jnp.float32),
            pltpu.SemaphoreType.DMA((3, n)),
            pltpu.SemaphoreType.DMA((3, n)),
            pltpu.SemaphoreType.DMA((3, n)),
        ],
        compiler_params=pltpu.CompilerParams(
            collective_id=0, has_side_effects=True, vmem_limit_bytes=56 * 1024 * 1024
        ),
    )(queries, keys, values, query_map, key_map, positions.reshape(1, tokens))


def solution(mesh):
    in_specs = (
        P("seq", "head"),
        P("seq", None),
        P("seq", None),
        P("head", None, None),
        P(),
        P("seq"),
    )
    return jax.shard_map(
        functools.partial(per_device, mesh.shape["seq"]),
        mesh=mesh, in_specs=in_specs, out_specs=P("seq", "head"), check_vma=False,
    )
```

```python
import functools
import math

import jax
import jax.numpy as jnp
from jax import lax
from jax.experimental import pallas as pl
from jax.experimental.pallas import tpu as pltpu
from jax.sharding import PartitionSpec as P

QHEADS = 128
KVH = 8
LENGTH = 131072
epsilon = 1e-06
masked_score = -1e30
MESH = pl.DeviceIdType.MESH
LOG2E = 1.4426950408889634
OWN_UNROLL = 8
UNROLL = 8
STEP_HEADS = 8


def elu_plus_one(x):
    return jnp.where(x > 0.0, x + 1.0, jnp.exp2(jnp.minimum(x, 0.0) * LOG2E))


def angle_parts(positions):
    angles = (0.5 * math.pi / LENGTH) * positions.astype(jnp.float32)
    return jnp.cos(angles), jnp.sin(angles)


def nt_dot(a, b):
    return lax.dot_general(a, b, (((1,), (1,)), ((), ())), preferred_element_type=jnp.float32)


def nn_dot(a, b):
    return jnp.dot(a, b, preferred_element_type=jnp.float32)


def causal_mask(size):
    row = lax.broadcasted_iota(jnp.int32, (size, size), 0)
    col = lax.broadcasted_iota(jnp.int32, (size, size), 1)
    return row >= col


def teacher_kernel(
    n, kv_local, per_group, own_unroll, unroll,
    q_hbm, k_hbm, v_hbm, kmap_ref, pos_ref,
    out_hbm, feats_ref, stacked_ref, cos_ref, sin_ref,
    q_ref, kbuf, vbuf, pbuf, acc, top, state, tbuf,
    local_sem, out_sem, send_sem, recv_sem, fwd_sem,
):
    tokens, hd = cos_ref.shape
    heads = kv_local * per_group
    nz = n // 2
    me = lax.axis_index("seq")
    z = me // 2
    core = me % 2
    partner = z * 2 + 1 - core
    group0 = lax.axis_index("head") * heads // (QHEADS // KVH)
    width = kv_local * hd
    columns = pl.ds(pl.multiple_of(group0 * hd, hd), width)
    scaling = LOG2E / math.sqrt(hd)

    local = (
        pltpu.make_async_copy(k_hbm.at[:, columns], kbuf.at[me], local_sem.at[0]),
        pltpu.make_async_copy(v_hbm.at[:, columns], vbuf.at[me], local_sem.at[1]),
        pltpu.make_async_copy(q_hbm, q_ref, local_sem.at[2]),
    )
    for copy in local:
        copy.start()

    barrier = pltpu.get_barrier_semaphore()

    def greet(zp, carry):
        pl.semaphore_signal(barrier, inc=1, device_id={"seq": zp * 2 + core}, device_id_type=MESH)
        return carry

    lax.fori_loop(0, z, greet, 0)
    lax.fori_loop(z + 1, nz, greet, 0)
    pl.semaphore_signal(barrier, inc=1, device_id={"seq": partner}, device_id_type=MESH)
    pl.semaphore_wait(barrier, nz)

    own = (k_hbm.at[:, columns], v_hbm.at[:, columns], pos_ref)
    buffers = (kbuf, vbuf, pbuf)

    def own_copy(part, slot, target):
        return pltpu.make_async_remote_copy(
            src_ref=own[part], dst_ref=buffers[part].at[me],
            send_sem=send_sem.at[part, slot], recv_sem=recv_sem.at[part, me],
            device_id={"seq": target}, device_id_type=MESH,
        )

    def forward_copy(part, zp):
        block = zp * 2 + core
        return pltpu.make_async_remote_copy(
            src_ref=buffers[part].at[block], dst_ref=buffers[part].at[block],
            send_sem=fwd_sem.at[part, zp], recv_sem=recv_sem.at[part, block],
            device_id={"seq": partner}, device_id_type=MESH,
        )

    def arrival(part, block):
        return pltpu.make_async_remote_copy(
            src_ref=buffers[part].at[block], dst_ref=buffers[part].at[block],
            send_sem=send_sem.at[part, 0], recv_sem=recv_sem.at[part, block],
            device_id={"seq": partner}, device_id_type=MESH,
        )

    @pl.when(core == 0)
    def _():
        for part in range(3):
            own_copy(part, z, partner).start()

    def send_up(zp, carry):
        for part in range(3):
            own_copy(part, zp, zp * 2 + core).start()
        return carry

    lax.fori_loop(z + 1, nz, send_up, 0)

    def take_and_forward(zp):
        @pl.when(zp >= 0)
        def _():
            for part in range(3):
                arrival(part, zp * 2 + core).wait_recv()
            for part in range(3):
                forward_copy(part, zp).start()

    def with_ones(values):
        return jnp.concatenate([values, jnp.ones(values.shape, jnp.bfloat16)], axis=1)

    def key_feats(keys, group, positions):
        cosine, sine = angle_parts(positions)
        projected = nn_dot(keys, kmap_ref[group0 + group]).T
        mapped = elu_plus_one(projected)
        return jnp.concatenate([cosine * mapped, sine * mapped], axis=0).astype(jnp.bfloat16)

    def query(h):
        return q_ref[:, pl.ds(pl.multiple_of(h * hd, hd), hd)]

    tall = jnp.broadcast_to(pos_ref[...].astype(jnp.float32), (hd, tokens)).T
    cosine, sine = angle_parts(tall)
    cos_ref[...] = cosine
    sin_ref[...] = sine
    for copy in local:
        copy.wait()

    tile = math.gcd(tokens, 128)
    for g in range(kv_local):
        group_cols = slice(g * hd, (g + 1) * hd)
        keys = kbuf[me, :, group_cols]
        values = with_ones(vbuf[me, :, group_cols])
        feats_ref[g] = key_feats(keys, g, pos_ref[...])
        state[g] = jnp.zeros((2 * hd, 2 * hd), jnp.float32)

        def own_body(i, carry, g=g, keys=keys, values=values):
            mask = causal_mask(tile)
            for u in range(own_unroll):
                h = g * per_group + i * own_unroll + u
                scores = nt_dot(query(h), keys)
                rows = []
                for t in range(0, tokens, tile):
                    pieces = [scores[t : t + tile, c : c + tile] * scaling for c in range(0, t + tile, tile)]
                    pieces[-1] = jnp.where(mask, pieces[-1], masked_score)
                    kept = jnp.concatenate(pieces, axis=1)
                    largest = jnp.max(kept, axis=1, keepdims=True)
                    part = jnp.exp2(kept - largest).astype(jnp.bfloat16)
                    if t + tile < tokens:
                        part = jnp.concatenate(
                            [part, jnp.zeros((tile, tokens - t - tile), jnp.bfloat16)], axis=1
                        )
                    rows.append(part)
                    top[h, t : t + tile, :] = jnp.broadcast_to(largest, (tile, hd))
                acc[h] = nn_dot(jnp.concatenate(rows, axis=0), values)
            return carry

        lax.fori_loop(0, per_group // own_unroll, own_body, 0)
        if g == 0:
            take_and_forward(z - 1)

    def use_blocks(first, count, per_step, following):
        span = count * tokens
        for g in range(kv_local):
            group_cols = slice(g * hd, (g + 1) * hd)
            keys = kbuf[pl.ds(first, count), :, group_cols].reshape(span, hd)
            values = with_ones(vbuf[pl.ds(first, count), :, group_cols].reshape(span, hd))
            positions = jnp.concatenate([pbuf[first + b] for b in range(count)], axis=1)
            state[g] += nn_dot(key_feats(keys, g, positions), values)

            def body(i, carry, g=g, keys=keys, values=values):
                for u in range(per_step):
                    h = g * per_group + i * per_step + u
                    scores = nt_dot(query(h), keys) * scaling
                    before = top[h]
                    largest = jnp.maximum(before, jnp.max(scores, axis=1, keepdims=True))
                    factor = jnp.exp2(before - largest)
                    wide = jnp.concatenate([largest] * (span // hd), axis=1)
                    weights = jnp.exp2(scores - wide).astype(jnp.bfloat16)
                    acc[h] = acc[h] * jnp.concatenate([factor, factor], axis=1) + nn_dot(weights, values)
                    top[h] = largest
                return carry

            lax.fori_loop(0, per_group // per_step, body, 0)
            if g == 0 and following is not None:
                take_and_forward(following)

    @pl.when(core == 1)
    def _():
        for part in range(3):
            arrival(part, partner).wait_recv()
        use_blocks(partner, 1, own_unroll, None)

    def step(i, carry):
        zp = z - 1 - i
        for part in range(3):
            arrival(part, zp * 2 + 1 - core).wait_recv()
        use_blocks(zp * 2, 2, unroll, zp - 1)
        return carry

    lax.fori_loop(0, z, step, 0)

    for g in range(kv_local):
        stacked_ref[g, :tokens, :] = with_ones(vbuf[me, :, g * hd : (g + 1) * hd])
        stacked_ref[g, tokens:, :] = state[g].astype(jnp.bfloat16)

        def last_body(i, carry, g=g):
            for u in range(own_unroll):
                h = g * per_group + i * own_unroll + u
                tbuf[:, pl.ds(pl.multiple_of(h * hd, hd), hd)] = (
                    acc[h, :, :hd] * reciprocal(acc[h, :, hd:])
                ).astype(jnp.bfloat16)
            return carry

        lax.fori_loop(0, per_group // own_unroll, last_body, 0)
        part_cols = pl.ds(g * per_group * hd, per_group * hd)
        pltpu.make_async_copy(tbuf.at[:, part_cols], out_hbm.at[:, part_cols], out_sem.at[g]).start()

    @pl.when(core == 0)
    def _():
        for part in range(3):
            own_copy(part, z, partner).wait_send()

    def sent(zp, carry):
        for part in range(3):
            own_copy(part, zp, zp * 2 + core).wait_send()
        return carry

    lax.fori_loop(z + 1, nz, sent, 0)

    def forwarded(zp, carry):
        for part in range(3):
            forward_copy(part, zp).wait_send()
        return carry

    lax.fori_loop(0, z, forwarded, 0)
    for g in range(kv_local):
        part_cols = pl.ds(g * per_group * hd, per_group * hd)
        pltpu.make_async_copy(tbuf.at[:, part_cols], out_hbm.at[:, part_cols], out_sem.at[g]).wait()


def reciprocal(x):
    guess = pl.reciprocal(x, approx=True)
    return guess * (2.0 - x * guess)


def student_kernel(step_heads, q_ref, qmap_ref, teacher_ref, feats_ref, stacked_ref, cos_ref, sin_ref, out_ref):
    tokens, hd = cos_ref.shape
    tile = math.gcd(tokens, 128)
    mask = causal_mask(tile)
    for u in range(step_heads):
        cols = slice(u * hd, (u + 1) * hd)
        mapped = elu_plus_one(nn_dot(q_ref[:, cols], qmap_ref[u]))
        qf = jnp.concatenate([cos_ref[...] * mapped, sin_ref[...] * mapped], axis=1).astype(jnp.bfloat16)
        inner = nn_dot(qf, feats_ref[0])
        rows = []
        for t in range(0, tokens, tile):
            pieces = [inner[t : t + tile, c : c + tile] for c in range(0, t + tile, tile)]
            pieces[-1] = jnp.where(mask, pieces[-1], 0.0)
            if t + tile < tokens:
                pieces.append(jnp.zeros((tile, tokens - t - tile), jnp.float32))
            rows.append(jnp.concatenate(pieces, axis=1).astype(jnp.bfloat16))
        both = nn_dot(jnp.concatenate([jnp.concatenate(rows, axis=0), qf], axis=1), stacked_ref[0])
        student = both[:, :hd] * reciprocal(both[:, hd:] + epsilon)
        out_ref[:, cols] = (2.0 * (student - teacher_ref[:, cols].astype(jnp.float32))).astype(jnp.bfloat16)


def per_device(n, queries, keys, values, query_map, key_map, positions):
    tokens = queries.shape[0]
    hd = key_map.shape[1]
    heads = query_map.shape[0]
    kv_local = max(1, heads // (QHEADS // KVH))
    per_group = heads // kv_local
    own_unroll = math.gcd(per_group, OWN_UNROLL)
    unroll = math.gcd(per_group, UNROLL)
    width = kv_local * hd
    vmem = pl.BlockSpec(memory_space=pltpu.VMEM)
    hbm = pl.BlockSpec(memory_space=pl.ANY)
    teacher, feats, stacked, cosine, sine = pl.pallas_call(
        functools.partial(teacher_kernel, n, kv_local, per_group, own_unroll, unroll),
        out_shape=(
            jax.ShapeDtypeStruct(queries.shape, jnp.bfloat16),
            jax.ShapeDtypeStruct((kv_local, 2 * hd, tokens), jnp.bfloat16),
            jax.ShapeDtypeStruct((kv_local, tokens + 2 * hd, 2 * hd), jnp.bfloat16),
            jax.ShapeDtypeStruct((tokens, hd), jnp.float32),
            jax.ShapeDtypeStruct((tokens, hd), jnp.float32),
        ),
        in_specs=[hbm, hbm, hbm, vmem, vmem],
        out_specs=[hbm, vmem, vmem, vmem, vmem],
        scratch_shapes=[
            pltpu.VMEM((tokens, heads * hd), jnp.bfloat16),
            pltpu.VMEM((n, tokens, width), jnp.bfloat16),
            pltpu.VMEM((n, tokens, width), jnp.bfloat16),
            pltpu.VMEM((n, 1, tokens), jnp.int32),
            pltpu.VMEM((heads, tokens, 2 * hd), jnp.float32),
            pltpu.VMEM((heads, tokens, hd), jnp.float32),
            pltpu.VMEM((kv_local, 2 * hd, 2 * hd), jnp.float32),
            pltpu.VMEM((tokens, heads * hd), jnp.bfloat16),
            pltpu.SemaphoreType.DMA((3,)),
            pltpu.SemaphoreType.DMA((kv_local,)),
            pltpu.SemaphoreType.DMA((3, n)),
            pltpu.SemaphoreType.DMA((3, n)),
            pltpu.SemaphoreType.DMA((3, n)),
        ],
        compiler_params=pltpu.CompilerParams(
            collective_id=0, has_side_effects=True, vmem_limit_bytes=56 * 1024 * 1024
        ),
    )(queries, keys, values, key_map, positions.reshape(1, tokens))

    step_heads = math.gcd(per_group, STEP_HEADS)
    by_columns = pl.BlockSpec((tokens, step_heads * hd), lambda i: (0, i))
    by_group = lambda rows, cols: pl.BlockSpec((1, rows, cols), lambda i: (i * step_heads // per_group, 0, 0))
    whole = pl.BlockSpec((tokens, hd), lambda i: (0, 0))
    return pl.pallas_call(
        functools.partial(student_kernel, step_heads),
        grid=(heads // step_heads,),
        out_shape=jax.ShapeDtypeStruct(queries.shape, jnp.bfloat16),
        in_specs=[
            by_columns,
            pl.BlockSpec((step_heads, hd, hd), lambda i: (i, 0, 0)),
            by_columns,
            by_group(2 * hd, tokens),
            by_group(tokens + 2 * hd, 2 * hd),
            whole,
            whole,
        ],
        out_specs=by_columns,
        compiler_params=pltpu.CompilerParams(vmem_limit_bytes=48 * 1024 * 1024),
    )(queries, query_map, teacher, feats, stacked, cosine, sine)


def solution(mesh):
    in_specs = (
        P("seq", "head"),
        P("seq", None),
        P("seq", None),
        P("head", None, None),
        P(),
        P("seq"),
    )
    return jax.shard_map(
        functools.partial(per_device, mesh.shape["seq"]),
        mesh=mesh, in_specs=in_specs, out_specs=P("seq", "head"), check_vma=False,
    )
```

```python
import functools
import math

import jax
import jax.numpy as jnp
from jax import lax
from jax.experimental import pallas as pl
from jax.experimental.pallas import tpu as pltpu
from jax.sharding import PartitionSpec as P

QHEADS = 128
KVH = 8
LENGTH = 131072
epsilon = 1e-06
masked_score = -1e30
MESH = pl.DeviceIdType.MESH
LOG2E = 1.4426950408889634
OWN_UNROLL = 16
UNROLL = 16
STEP_HEADS = 16


def elu_plus_one(x):
    return jnp.where(x > 0.0, x + 1.0, jnp.exp2(jnp.minimum(x, 0.0) * LOG2E))


def angle_parts(positions):
    angles = (0.5 * math.pi / LENGTH) * positions.astype(jnp.float32)
    return jnp.cos(angles), jnp.sin(angles)


def nt_dot(a, b):
    return lax.dot_general(a, b, (((1,), (1,)), ((), ())), preferred_element_type=jnp.float32)


def nn_dot(a, b):
    return jnp.dot(a, b, preferred_element_type=jnp.float32)


def causal_mask(size):
    row = lax.broadcasted_iota(jnp.int32, (size, size), 0)
    col = lax.broadcasted_iota(jnp.int32, (size, size), 1)
    return row >= col


def teacher_kernel(
    n, kv_local, per_group, own_unroll, unroll,
    q_hbm, k_hbm, v_hbm, kmap_ref, pos_ref,
    out_hbm, feats_ref, stacked_ref, cos_ref, sin_ref,
    q_ref, kbuf, vbuf, pbuf, acc, top, state, tbuf,
    local_sem, out_sem, send_sem, recv_sem, fwd_sem,
):
    tokens, hd = cos_ref.shape
    heads = kv_local * per_group
    nz = n // 2
    me = lax.axis_index("seq")
    z = me // 2
    core = me % 2
    partner = z * 2 + 1 - core
    group0 = lax.axis_index("head") * heads // (QHEADS // KVH)
    width = kv_local * hd
    columns = pl.ds(pl.multiple_of(group0 * hd, hd), width)
    scaling = LOG2E / math.sqrt(hd)

    local = (
        pltpu.make_async_copy(k_hbm.at[:, columns], kbuf.at[me], local_sem.at[0]),
        pltpu.make_async_copy(v_hbm.at[:, columns], vbuf.at[me], local_sem.at[1]),
        pltpu.make_async_copy(q_hbm, q_ref, local_sem.at[2]),
    )
    for copy in local:
        copy.start()

    barrier = pltpu.get_barrier_semaphore()

    def greet(zp, carry):
        pl.semaphore_signal(barrier, inc=1, device_id={"seq": zp * 2 + core}, device_id_type=MESH)
        return carry

    lax.fori_loop(0, z, greet, 0)
    lax.fori_loop(z + 1, nz, greet, 0)
    pl.semaphore_signal(barrier, inc=1, device_id={"seq": partner}, device_id_type=MESH)
    pl.semaphore_wait(barrier, nz)

    own = (k_hbm.at[:, columns], v_hbm.at[:, columns], pos_ref)
    buffers = (kbuf, vbuf, pbuf)

    def own_copy(part, slot, target):
        return pltpu.make_async_remote_copy(
            src_ref=own[part], dst_ref=buffers[part].at[me],
            send_sem=send_sem.at[part, slot], recv_sem=recv_sem.at[part, me],
            device_id={"seq": target}, device_id_type=MESH,
        )

    def forward_copy(part, zp):
        block = zp * 2 + core
        return pltpu.make_async_remote_copy(
            src_ref=buffers[part].at[block], dst_ref=buffers[part].at[block],
            send_sem=fwd_sem.at[part, zp], recv_sem=recv_sem.at[part, block],
            device_id={"seq": partner}, device_id_type=MESH,
        )

    def arrival(part, block):
        return pltpu.make_async_remote_copy(
            src_ref=buffers[part].at[block], dst_ref=buffers[part].at[block],
            send_sem=send_sem.at[part, 0], recv_sem=recv_sem.at[part, block],
            device_id={"seq": partner}, device_id_type=MESH,
        )

    @pl.when(core == 0)
    def _():
        for part in range(3):
            own_copy(part, z, partner).start()

    def send_up(zp, carry):
        for part in range(3):
            own_copy(part, zp, zp * 2 + core).start()
        return carry

    lax.fori_loop(z + 1, nz, send_up, 0)

    def take_and_forward(zp):
        @pl.when(zp >= 0)
        def _():
            for part in range(3):
                arrival(part, zp * 2 + core).wait_recv()
            for part in range(3):
                forward_copy(part, zp).start()

    def with_ones(values):
        return jnp.concatenate([values, jnp.ones(values.shape, jnp.bfloat16)], axis=1)

    def key_feats(keys, group, positions):
        cosine, sine = angle_parts(positions)
        projected = nn_dot(keys, kmap_ref[group0 + group]).T
        mapped = elu_plus_one(projected)
        return jnp.concatenate([cosine * mapped, sine * mapped], axis=0).astype(jnp.bfloat16)

    def query(h):
        return q_ref[:, pl.ds(pl.multiple_of(h * hd, hd), hd)]

    tall = jnp.broadcast_to(pos_ref[...].astype(jnp.float32), (hd, tokens)).T
    cosine, sine = angle_parts(tall)
    cos_ref[...] = cosine
    sin_ref[...] = sine
    for copy in local:
        copy.wait()

    tile = math.gcd(tokens, 128)
    for g in range(kv_local):
        group_cols = slice(g * hd, (g + 1) * hd)
        keys = kbuf[me, :, group_cols]
        values = with_ones(vbuf[me, :, group_cols])
        feats_ref[g] = key_feats(keys, g, pos_ref[...])
        state[g] = jnp.zeros((2 * hd, 2 * hd), jnp.float32)

        def own_body(i, carry, g=g, keys=keys, values=values):
            mask = causal_mask(tile)
            for u in range(own_unroll):
                h = g * per_group + i * own_unroll + u
                scores = nt_dot(query(h), keys)
                rows = []
                for t in range(0, tokens, tile):
                    pieces = [scores[t : t + tile, c : c + tile] * scaling for c in range(0, t + tile, tile)]
                    pieces[-1] = jnp.where(mask, pieces[-1], masked_score)
                    kept = jnp.concatenate(pieces, axis=1)
                    largest = jnp.max(kept, axis=1, keepdims=True)
                    part = jnp.exp2(kept - largest).astype(jnp.bfloat16)
                    if t + tile < tokens:
                        part = jnp.concatenate(
                            [part, jnp.zeros((tile, tokens - t - tile), jnp.bfloat16)], axis=1
                        )
                    rows.append(part)
                    top[h, t : t + tile, :] = jnp.broadcast_to(largest, (tile, hd))
                acc[h] = nn_dot(jnp.concatenate(rows, axis=0), values)
            return carry

        lax.fori_loop(0, per_group // own_unroll, own_body, 0)
        if g == 0:
            take_and_forward(z - 1)

    def use_blocks(first, count, per_step, following):
        span = count * tokens
        for g in range(kv_local):
            group_cols = slice(g * hd, (g + 1) * hd)
            keys = kbuf[pl.ds(first, count), :, group_cols].reshape(span, hd)
            values = with_ones(vbuf[pl.ds(first, count), :, group_cols].reshape(span, hd))
            positions = jnp.concatenate([pbuf[first + b] for b in range(count)], axis=1)
            state[g] += nn_dot(key_feats(keys, g, positions), values)

            def body(i, carry, g=g, keys=keys, values=values):
                for u in range(per_step):
                    h = g * per_group + i * per_step + u
                    scores = nt_dot(query(h), keys) * scaling
                    before = top[h]
                    largest = jnp.maximum(before, jnp.max(scores, axis=1, keepdims=True))
                    factor = jnp.exp2(before - largest)
                    wide = jnp.concatenate([largest] * (span // hd), axis=1)
                    weights = jnp.exp2(scores - wide).astype(jnp.bfloat16)
                    acc[h] = acc[h] * jnp.concatenate([factor, factor], axis=1) + nn_dot(weights, values)
                    top[h] = largest
                return carry

            lax.fori_loop(0, per_group // per_step, body, 0)
            if g == 0 and following is not None:
                take_and_forward(following)

    @pl.when(core == 1)
    def _():
        for part in range(3):
            arrival(part, partner).wait_recv()
        use_blocks(partner, 1, own_unroll, None)

    def step(i, carry):
        zp = z - 1 - i
        for part in range(3):
            arrival(part, zp * 2 + 1 - core).wait_recv()
        use_blocks(zp * 2, 2, unroll, zp - 1)
        return carry

    lax.fori_loop(0, z, step, 0)

    for g in range(kv_local):
        stacked_ref[g, :tokens, :] = with_ones(vbuf[me, :, g * hd : (g + 1) * hd])
        stacked_ref[g, tokens:, :] = state[g].astype(jnp.bfloat16)

        def last_body(i, carry, g=g):
            for u in range(own_unroll):
                h = g * per_group + i * own_unroll + u
                tbuf[:, pl.ds(pl.multiple_of(h * hd, hd), hd)] = (
                    acc[h, :, :hd] * reciprocal(acc[h, :, hd:])
                ).astype(jnp.bfloat16)
            return carry

        lax.fori_loop(0, per_group // own_unroll, last_body, 0)
        part_cols = pl.ds(g * per_group * hd, per_group * hd)
        pltpu.make_async_copy(tbuf.at[:, part_cols], out_hbm.at[:, part_cols], out_sem.at[g]).start()

    @pl.when(core == 0)
    def _():
        for part in range(3):
            own_copy(part, z, partner).wait_send()

    def sent(zp, carry):
        for part in range(3):
            own_copy(part, zp, zp * 2 + core).wait_send()
        return carry

    lax.fori_loop(z + 1, nz, sent, 0)

    def forwarded(zp, carry):
        for part in range(3):
            forward_copy(part, zp).wait_send()
        return carry

    lax.fori_loop(0, z, forwarded, 0)
    for g in range(kv_local):
        part_cols = pl.ds(g * per_group * hd, per_group * hd)
        pltpu.make_async_copy(tbuf.at[:, part_cols], out_hbm.at[:, part_cols], out_sem.at[g]).wait()


def reciprocal(x):
    guess = pl.reciprocal(x, approx=True)
    return guess * (2.0 - x * guess)


def student_kernel(step_heads, q_ref, qmap_ref, teacher_ref, feats_ref, stacked_ref, cos_ref, sin_ref, out_ref):
    tokens, hd = cos_ref.shape
    tile = math.gcd(tokens, 128)
    mask = causal_mask(tile)
    for u in range(step_heads):
        cols = slice(u * hd, (u + 1) * hd)
        mapped = elu_plus_one(nn_dot(q_ref[:, cols], qmap_ref[u]))
        qf = jnp.concatenate([cos_ref[...] * mapped, sin_ref[...] * mapped], axis=1).astype(jnp.bfloat16)
        inner = nn_dot(qf, feats_ref[0])
        rows = []
        for t in range(0, tokens, tile):
            pieces = [inner[t : t + tile, c : c + tile] for c in range(0, t + tile, tile)]
            pieces[-1] = jnp.where(mask, pieces[-1], 0.0)
            if t + tile < tokens:
                pieces.append(jnp.zeros((tile, tokens - t - tile), jnp.float32))
            rows.append(jnp.concatenate(pieces, axis=1).astype(jnp.bfloat16))
        both = nn_dot(jnp.concatenate([jnp.concatenate(rows, axis=0), qf], axis=1), stacked_ref[0])
        student = both[:, :hd] * reciprocal(both[:, hd:] + epsilon)
        out_ref[:, cols] = (2.0 * (student - teacher_ref[:, cols].astype(jnp.float32))).astype(jnp.bfloat16)


def per_device(n, queries, keys, values, query_map, key_map, positions):
    tokens = queries.shape[0]
    hd = key_map.shape[1]
    heads = query_map.shape[0]
    kv_local = max(1, heads // (QHEADS // KVH))
    per_group = heads // kv_local
    own_unroll = math.gcd(per_group, OWN_UNROLL)
    unroll = math.gcd(per_group, UNROLL)
    width = kv_local * hd
    vmem = pl.BlockSpec(memory_space=pltpu.VMEM)
    hbm = pl.BlockSpec(memory_space=pl.ANY)
    teacher, feats, stacked, cosine, sine = pl.pallas_call(
        functools.partial(teacher_kernel, n, kv_local, per_group, own_unroll, unroll),
        out_shape=(
            jax.ShapeDtypeStruct(queries.shape, jnp.bfloat16),
            jax.ShapeDtypeStruct((kv_local, 2 * hd, tokens), jnp.bfloat16),
            jax.ShapeDtypeStruct((kv_local, tokens + 2 * hd, 2 * hd), jnp.bfloat16),
            jax.ShapeDtypeStruct((tokens, hd), jnp.float32),
            jax.ShapeDtypeStruct((tokens, hd), jnp.float32),
        ),
        in_specs=[hbm, hbm, hbm, vmem, vmem],
        out_specs=[hbm, vmem, vmem, vmem, vmem],
        scratch_shapes=[
            pltpu.VMEM((tokens, heads * hd), jnp.bfloat16),
            pltpu.VMEM((n, tokens, width), jnp.bfloat16),
            pltpu.VMEM((n, tokens, width), jnp.bfloat16),
            pltpu.VMEM((n, 1, tokens), jnp.int32),
            pltpu.VMEM((heads, tokens, 2 * hd), jnp.float32),
            pltpu.VMEM((heads, tokens, hd), jnp.float32),
            pltpu.VMEM((kv_local, 2 * hd, 2 * hd), jnp.float32),
            pltpu.VMEM((tokens, heads * hd), jnp.bfloat16),
            pltpu.SemaphoreType.DMA((3,)),
            pltpu.SemaphoreType.DMA((kv_local,)),
            pltpu.SemaphoreType.DMA((3, n)),
            pltpu.SemaphoreType.DMA((3, n)),
            pltpu.SemaphoreType.DMA((3, n)),
        ],
        compiler_params=pltpu.CompilerParams(
            collective_id=0, has_side_effects=True, vmem_limit_bytes=61 * 1024 * 1024
        ),
    )(queries, keys, values, key_map, positions.reshape(1, tokens))

    step_heads = math.gcd(per_group, STEP_HEADS)
    by_columns = pl.BlockSpec((tokens, step_heads * hd), lambda i: (0, i))
    by_group = lambda rows, cols: pl.BlockSpec((1, rows, cols), lambda i: (i * step_heads // per_group, 0, 0))
    whole = pl.BlockSpec((tokens, hd), lambda i: (0, 0))
    return pl.pallas_call(
        functools.partial(student_kernel, step_heads),
        grid=(heads // step_heads,),
        out_shape=jax.ShapeDtypeStruct(queries.shape, jnp.bfloat16),
        in_specs=[
            by_columns,
            pl.BlockSpec((step_heads, hd, hd), lambda i: (i, 0, 0)),
            by_columns,
            by_group(2 * hd, tokens),
            by_group(tokens + 2 * hd, 2 * hd),
            whole,
            whole,
        ],
        out_specs=by_columns,
        compiler_params=pltpu.CompilerParams(vmem_limit_bytes=61 * 1024 * 1024),
    )(queries, query_map, teacher, feats, stacked, cosine, sine)


def solution(mesh):
    in_specs = (
        P("seq", "head"),
        P("seq", None),
        P("seq", None),
        P("head", None, None),
        P(),
        P("seq"),
    )
    return jax.shard_map(
        functools.partial(per_device, mesh.shape["seq"]),
        mesh=mesh, in_specs=in_specs, out_specs=P("seq", "head"), check_vma=False,
    )
```
